256 devices in a mesh: island: 32 (over x_hi, z, core), zero: 8 (over y, x_lo).
Axes of the slice: x: 4 (x_hi: 2, x_lo: 2; x = x_hi * 2 + x_lo), y: 4, z: 8, core: 2. Of those that a mesh axis runs over, the one named last changes fastest.
Arguments:
- params: float32 [32, 2048, 2048], P('island', 'zero'), may hold values from -6 to 6
- moment: bfloat16 [32, 2048, 2048], P('island', 'zero'), may hold values from -4 to 4
- second: bfloat16 [32, 2048, 2048], P('island', 'zero'), may hold values from 0.5 to 4
- active: bfloat16 [32, 4096, 2048], P('island', 'zero'), may hold values from -6 to 6
- target: bfloat16 [32, 4096, 2048], P('island', 'zero'), may hold values from -6 to 6
- row_ids: int32 [2, 32, 2048], P(None, 'island', 'zero'), may hold values from 0 to 511
- step_index: int32 [1], replicated, may hold values from 0 to 999
Outputs:
- params_out: float32 [32, 2048, 2048], P('island', 'zero')
- moment_out: bfloat16 [32, 2048, 2048], P('island', 'zero')
- second_out: bfloat16 [32, 2048, 2048], P('island', 'zero')
The draws below stay inside these ranges and needn't reach their ends.
All inputs are finite; a program needn't handle non-finite values.
Results may differ from the reference program's by a relative error of at most 0.02.
Values may be sent and summed in bfloat16 or wider, within the bound.
A program may use at most 128 MiB of HBM per device.

```python
import math
import jax
import jax.numpy as jnp
from jax import lax

D = 2048
QW = 2048
TOK = 256
ROWS = 512
ITERS = 2
ISL = 32
TOK_ISL = 2048
ROWS_ISL = 4096
N_ISLAND = 32
N_ZERO = 8


def place_ends(array, key, low, top_value):
    extent = array.shape
    spot = [jax.random.randint(jax.random.fold_in(key, axis), (), 0, extent[axis]) for axis in range(len(extent))]
    array = array.at[tuple(spot)].set(low)
    longest = extent.index(max(extent))
    spot[longest] = (spot[longest] + 1) % extent[longest]
    return array.at[tuple(spot)].set(top_value)


def block_scale(rng, extent, split, low, largest):
    factor_of, own = 1.0, jax.random.fold_in(rng, 6)
    for dim, parts in split:
        heights = jnp.exp(jax.random.uniform(jax.random.fold_in(own, dim), (parts,), jnp.float32, low / len(split), largest / len(split)))
        factor_of = factor_of * jnp.repeat(heights, extent[dim] // parts).reshape([-1 if axis == dim else 1 for axis in range(len(extent))])
    return factor_of


def scatter_about(own_key, dims, width, reach, split=(), kind=jnp.bfloat16):
    result = jax.random.normal(own_key, dims, jnp.float32) * width
    if len(split) > 0:
        result = block_scale(own_key, dims, split, -0.22, 0.18) * result
    return jnp.clip(result, min=-reach, max=reach).astype(kind)


def setup_inputs(seed: int = 0) -> dict:
    streams_of = jax.random.split(jax.random.key(seed), 8)
    return {
        "params": scatter_about(streams_of[0], (ISL, D, QW), 1.0, 6.0, ((0, 32), (1, 8)), jnp.float32),
        "moment": scatter_about(streams_of[1], (ISL, D, QW), 0.5, 4.0, ((0, 32), (1, 8))),
        "second": jnp.clip(jnp.exp(math.log(4.0) - 2.0794415 * jax.random.uniform(streams_of[2], (ISL, D, QW), jnp.float32) ** block_scale(streams_of[2], (ISL, D, QW), ((0, 32), (1, 8)), -0.2, 0.2)), 0.5, 4.0).astype(jnp.bfloat16),
        "active": scatter_about(streams_of[3], (ISL, ROWS_ISL, D), 1.0, 6.0, ((0, 32), (1, 8))),
        "target": scatter_about(streams_of[4], (ISL, ROWS_ISL, QW), 1.0, 6.0, ((0, 32), (1, 8))),
        "row_ids": place_ends(jax.random.randint(streams_of[5], (ITERS, ISL, TOK_ISL), 0, ROWS), jax.random.fold_in(streams_of[5], 1), 0, ROWS - 1).astype(jnp.int32),
        "step_index": jax.random.randint(streams_of[6], (1,), 0, 1000).astype(jnp.int32),
    }


beta_mean = 0.9
beta_square = 0.95
step_rate = 0.02
epsilon_add = 1e-08
gossip_rate = 0.4

def cosine_table():
    places = jnp.arange(128, dtype=jnp.float32)[:, None]
    orders = jnp.arange(64, dtype=jnp.float32)[None, :]
    cosines = jnp.cos(math.pi * (places + 0.5) * orders / 128.0) * math.sqrt(2.0 / 128.0)
    return jnp.where(orders == 0.0, cosines * math.sqrt(0.5), cosines)

def compress(values, cosines):
    blocks = values.reshape(values.shape[:-1] + (-1, 128))
    coeffs = jnp.einsum('...bi,ik->...bk', blocks, cosines, precision=lax.Precision.HIGHEST)
    return coeffs.reshape(values.shape[:-1] + (-1,))

def expand(coeffs, cosines):
    blocks = coeffs.reshape(coeffs.shape[:-1] + (-1, 64))
    values = jnp.einsum('...bk,ik->...bi', blocks, cosines, precision=lax.Precision.HIGHEST)
    return values.reshape(coeffs.shape[:-1] + (-1,))

def island_step(operands, cosines):
    master, mean_old, square_old, leftover, active, target, chosen_all = operands
    weights = master.astype(jnp.bfloat16)
    summed = jnp.zeros(master.shape, jnp.float32)
    for device in range(N_ZERO):
        chosen = chosen_all[device * TOK:(device + 1) * TOK] + device * ROWS
        inputs = jnp.take(active, chosen, axis=0)
        wanted = jnp.take(target, chosen, axis=0)
        output = jnp.dot(inputs, weights, preferred_element_type=jnp.float32)
        residual = (output - wanted.astype(jnp.float32)).astype(jnp.bfloat16)
        partial_term = jnp.dot(inputs.T, residual, preferred_element_type=jnp.float32).astype(jnp.bfloat16)
        summed = summed + lax.optimization_barrier(partial_term).astype(jnp.float32)
    grad = summed * (1.0 / math.sqrt(D * TOK_ISL))
    mean_next = beta_mean * mean_old.astype(jnp.float32) + (1.0 - beta_mean) * grad
    square_next = beta_square * square_old.astype(jnp.float32) + (1.0 - beta_square) * grad * grad
    updated = master - step_rate * mean_next / (jnp.sqrt(square_next) + epsilon_add)
    carried = updated + leftover
    coeffs = compress(carried, cosines).astype(jnp.bfloat16)
    leftover_next = carried - expand(coeffs.astype(jnp.float32), cosines)
    return (updated, mean_next.astype(jnp.bfloat16), square_next.astype(jnp.bfloat16), coeffs, leftover_next)

def reference(params, moment, second, active, target, row_ids, step_index):
    cosines = cosine_table()
    levels = N_ISLAND.bit_length() - 1
    leftover = jnp.zeros(params.shape, jnp.float32)
    for iteration in range(ITERS):
        operands = (params, moment, second, leftover, active, target, row_ids[iteration])
        updated, moment, second, coeffs, leftover = lax.map(lambda items: island_step(items, cosines), operands)
        degree = jnp.remainder(step_index[0] + iteration, levels).astype(jnp.int32)
        stride = jnp.left_shift(jnp.int32(1), degree).astype(jnp.int32)
        partner = jnp.bitwise_xor(jnp.arange(N_ISLAND, dtype=jnp.int32), stride).astype(jnp.int32)
        remote = jnp.take(coeffs, partner, axis=0)
        params = updated + gossip_rate * expand(remote.astype(jnp.float32) - coeffs.astype(jnp.float32), cosines)
    return (params, moment, second)
```

```python
import functools
import math

import jax
import jax.numpy as jnp
import numpy as np
from jax import lax
from jax.experimental import pallas as pl
from jax.experimental.pallas import tpu as pltpu
from jax.sharding import PartitionSpec as P

MESH = pl.DeviceIdType.MESH
BF16 = jnp.bfloat16
F32 = jnp.float32

ITERS = 2
NY = 4
NX = 2
S = 4

beta_mean = 0.9
beta_square = 0.95
step_rate = 0.02
epsilon_add = 1e-08
gossip_rate = 0.4


def cosine_tables():
    places = np.arange(128)[:, None]
    orders = np.arange(64)[None, :]
    one = np.cos(math.pi * (places + 0.5) * orders / 128.0) * math.sqrt(2.0 / 128.0)
    one = np.where(orders == 0, one * math.sqrt(0.5), one)
    two = np.zeros((256, 128))
    two[:128, :64] = one
    two[128:, 64:] = one
    two = two.astype(np.float32)
    high = two.astype(jnp.bfloat16)
    low = (two - high.astype(np.float32)).astype(jnp.bfloat16)
    return high, low, np.ascontiguousarray(high.T), np.ascontiguousarray(low.T)


def dot(a, b):
    return jnp.dot(a, b, preferred_element_type=F32)


def kernel(
    bits,
    params_in, moment_in, second_in, act, tgt, ids, ch, cl, eh, el,
    params_out, moment_out, second_out,
    master, mean, square, left, x_all, x_turn, y_send, y_all, w_send, w_all,
    res, own, gx_send, gx_recv, gy_send, gy_recv, c_send, c_recv,
    in_sem, out_sem,
    xa_s, xa_r, ya_s, ya_r, wy_s, wy_r, wx_s, wx_r, gx_s, gx_r, gy_s, gy_r, c_s, c_r,
):
    rows, width = master.shape
    tokens = ids.shape[1]
    stored = act.shape[0]
    depth = act.shape[1]
    chunk = width // S
    part = chunk // NY
    half = depth // NX
    island = lax.axis_index("island")
    z = lax.axis_index("zero")
    x = lax.rem(z, NX)
    y = lax.div(z, NX)
    other = 1 - x
    factor = 1.0 / math.sqrt(depth * tokens * NX * NY)

    def along_y(dy):
        return (island, lax.rem(y + dy, NY) * NX + x)

    across = (island, y * NX + other)
    partners = []
    for bit in bits:
        apart = 2**bit
        partners.append((island + apart * (1 - 2 * lax.rem(lax.div(island, apart), 2)), z))

    barrier = pltpu.get_barrier_semaphore()
    friends = [along_y(1), along_y(2), along_y(3), across] + partners
    for friend in friends:
        pl.semaphore_signal(barrier, inc=1, device_id=friend, device_id_type=MESH)

    started = []

    def send(src, dst, s_sem, r_sem, device):
        copy = pltpu.make_async_remote_copy(
            src_ref=src, dst_ref=dst, send_sem=s_sem, recv_sem=r_sem,
            device_id=device, device_id_type=MESH,
        )
        copy.start()
        started.append(copy)
        return copy

    loads = []
    for s in range(S):
        cols = pl.ds(s * chunk, chunk)
        loads.append(pltpu.make_async_copy(params_in.at[:, cols], master.at[:, cols], in_sem.at[s]))
    loads.append(pltpu.make_async_copy(moment_in, mean, in_sem.at[S]))
    loads.append(pltpu.make_async_copy(second_in, square, in_sem.at[S + 1]))
    for load in loads:
        load.start()

    def selector(k):
        spots = lax.broadcasted_iota(jnp.int32, (stored, tokens), 0)
        return jnp.where(spots == ids[k : k + 1, :], 1.0, 0.0).astype(F32).T.astype(BF16)

    def pick_x(k):
        pick = selector(k)
        for b in range(NX * NY):
            to = (b % NX) * NY + b // NX
            block = dot(pick, act[:, b * rows : (b + 1) * rows])
            x_all[k, 0:tokens, to * rows : (to + 1) * rows] = block.astype(BF16)

    def pick_y(k):
        pick = selector(k)
        for s in range(S):
            block = dot(pick, tgt[:, s * chunk : (s + 1) * chunk]).astype(BF16)
            for q in range(NY):
                y_send[k, s, q] = block[:, q * part : (q + 1) * part]

    def turn(k, slot):
        def step(b, _):
            at = pl.multiple_of(b * rows, rows)
            block = x_all[k, slot * tokens : (slot + 1) * tokens, pl.ds(at, rows)]
            x_turn[k, pl.ds(at, rows), slot * tokens : (slot + 1) * tokens] = block.T
            return 0

        lax.fori_loop(0, depth // rows, step, 0)

    upper = pl.ds(0, tokens // 2)
    lower = pl.ds(tokens // 2, tokens // 2)

    def x_rows(k, slot, which):
        return x_all.at[k, pl.ds(slot * tokens + which * (tokens // 2), tokens // 2)]

    xs = {}

    def x_first(k):
        for n, (which, dy, slot) in enumerate(((0, 1, 1), (1, 3, 2), (1, 1, 1), (0, 3, 2))):
            xs[k, n] = send(
                x_rows(k, 0, which), x_rows(k, slot, which), xa_s.at[k, n], xa_r.at[k, n], along_y(dy)
            )

    def x_second(k):
        xs[k, 0].wait_recv()
        xs[k, 4] = send(x_rows(k, 1, 0), x_rows(k, 3, 0), xa_s.at[k, 4], xa_r.at[k, 4], along_y(1))
        xs[k, 1].wait_recv()
        xs[k, 5] = send(x_rows(k, 2, 1), x_rows(k, 3, 1), xa_s.at[k, 5], xa_r.at[k, 5], along_y(3))

    def x_last(k):
        xs[k, 2].wait_recv()
        turn(k, 1)
        xs[k, 3].wait_recv()
        turn(k, 2)
        xs[k, 4].wait_recv()
        xs[k, 5].wait_recv()
        turn(k, 3)

    slot_of = {1: 1, 3: 2, 2: 3}
    ys, wys, wxs, gxs, gys, cs = {}, {}, {}, {}, {}, {}

    def y_first(k, s):
        for n, dy in enumerate((1, 3, 2)):
            ys[k, s, n] = send(
                y_send.at[k, s, lax.rem(y + dy, NY)], y_all.at[k, s, slot_of[dy]],
                ya_s.at[k, s, n], ya_r.at[k, s, n], along_y(dy),
            )
        y_all[k, s, 0] = y_send[k, s, y]

    def w_first(k, s):
        for q in range(NY):
            at = s * chunk + q * part
            w_send[k, s, q] = master[:, at : at + part].astype(BF16)
        mine = pl.ds(pl.multiple_of((x * NY + y) * rows, rows), rows)
        for n, dy in enumerate((1, 3, 2)):
            wys[k, s, n] = send(
                w_send.at[k, s, lax.rem(y + dy, NY)], w_all.at[k, s, mine],
                wy_s.at[k, s, n], wy_r.at[k, s, n], along_y(dy),
            )
        w_all[k, s, mine] = w_send[k, s, y]

    def w_second(k, s):
        for n in range(3):
            wys[k, s, n].wait_recv()
        mine = w_all.at[k, s, pl.ds(pl.multiple_of(x * half, half), half)]
        wxs[k, s] = send(mine, mine, wx_s.at[k, s], wx_r.at[k, s], across)

    def work(k, s):
        if s == 0:
            x_last(k)
        for n in range(3):
            ys[k, s, n].wait_recv()
        wxs[k, s].wait_recv()
        for slot in range(NY):
            at = slot * tokens
            out = dot(x_all[k, at : at + tokens, :], w_all[k, s])
            res[at : at + tokens, :] = (out - y_all[k, s, slot].astype(F32)).astype(BF16)

        def term(side, b):
            at = pl.multiple_of(side * half + b * rows, rows)
            return dot(x_turn[k, pl.ds(at, rows), :], res[...])

        for b in range(NY):
            gx_send[k, s, b] = term(other, b).astype(BF16)
        gxs[k, s] = send(gx_send.at[k, s], gx_recv.at[k, s], gx_s.at[k, s], gx_r.at[k, s], across)
        for b in range(NY):
            own[s, b] = term(x, b)

    def add(k, s):
        gxs[k, s].wait_recv()
        for b in range(NY):
            gy_send[k, s, b] = (own[s, b] + gx_recv[k, s, b].astype(F32)).astype(BF16)
        for n, dy in enumerate((1, 3, 2)):
            gys[k, s, n] = send(
                gy_send.at[k, s, lax.rem(y + dy, NY)], gy_recv.at[k, s, y],
                gy_s.at[k, s, n], gy_r.at[k, s, n], along_y(dy),
            )
        gy_recv[k, s, y] = gy_send[k, s, y]

    def expand(c):
        return dot(c, eh[...]) + dot(c, el[...])

    def update(k, s):
        for n in range(3):
            gys[k, s, n].wait_recv()
        if k == 0 and s == 0:
            loads[S].wait()
            loads[S + 1].wait()
        wide = 256
        for j in range(chunk // wide):
            at = s * chunk + j * wide
            cols = slice(at, at + wide)
            per = wide // part
            grad = jnp.concatenate([gy_recv[k, s, j * per + q] for q in range(per)], axis=1)
            grad = grad.astype(F32) * factor
            mean_next = beta_mean * mean[:, cols].astype(F32) + (1.0 - beta_mean) * grad
            square_next = beta_square * square[:, cols].astype(F32) + (1.0 - beta_square) * grad * grad
            mean[:, cols] = mean_next.astype(BF16)
            square[:, cols] = square_next.astype(BF16)
            updated = master[:, cols] - step_rate * mean_next / (jnp.sqrt(square_next) + epsilon_add)
            carried = updated if k == 0 else updated + left[:, cols]
            high = carried.astype(BF16)
            low = (carried - high.astype(F32)).astype(BF16)
            coeffs = (dot(high, ch[...]) + (dot(low, ch[...]) + dot(high, cl[...]))).astype(BF16)
            c_send[k, s, :, j * (wide // 2) : (j + 1) * (wide // 2)] = coeffs
            back = expand(coeffs)
            if k + 1 < ITERS:
                left[:, cols] = carried - back
            master[:, cols] = updated - gossip_rate * back
        cs[k, s] = send(c_send.at[k, s], c_recv.at[k, s], c_s.at[k, s], c_r.at[k, s], partners[k])
        if k + 1 == ITERS:
            put(mean, moment_out, s, 1)
            put(square, second_out, s, 2)

    stores = []

    def put(src, dst, s, n):
        cols = pl.ds(s * chunk, chunk)
        copy = pltpu.make_async_copy(src.at[:, cols], dst.at[:, cols], out_sem.at[n, s])
        copy.start()
        stores.append(copy)

    def gossip(k, s):
        cs[k, s].wait_recv()
        wide = 256
        for j in range(chunk // wide):
            at = s * chunk + j * wide
            remote = c_recv[k, s, :, j * (wide // 2) : (j + 1) * (wide // 2)]
            master[:, at : at + wide] = master[:, at : at + wide] + gossip_rate * expand(remote)
        if k + 1 == ITERS:
            put(master, params_out, s, 0)
        else:
            w_first(k + 1, s)

    pick_x(0)
    loads[0].wait()
    pl.semaphore_wait(barrier, len(friends))
    w_first(0, 0)
    x_first(0)
    pick_y(0)
    y_first(0, 0)
    turn(0, 0)
    w_second(0, 0)
    x_second(0)
    for s in range(1, S):
        loads[s].wait()
        w_first(0, s)
        y_first(0, s)
    pick_x(1)
    pick_y(1)
    turn(1, 0)

    stages = [w_second, work, add, update, gossip]
    line = [(stage, k) for k in range(ITERS) for stage in stages]
    for t in range(len(line) + S - 1):
        if t == 2:
            x_first(1)
        if t == 4:
            x_second(1)
            for s in range(S):
                y_first(1, s)
        for s in range(S):
            if 0 <= t - s < len(line):
                stage, k = line[t - s]
                if (stage, k, s) != (w_second, 0, 0):
                    stage(k, s)

    for copy in started:
        copy.wait_send()
    for copy in stores:
        copy.wait()


def window(bits, collective_id, params, moment, second, active, target, ids, tables):
    rows, width = params.shape
    depth = active.shape[1]
    tokens = ids.shape[1]
    chunk = width // S
    part = chunk // NY
    group = tokens * NY
    half = depth // NX
    vmem = pl.BlockSpec(memory_space=pltpu.VMEM)
    anywhere = pl.BlockSpec(memory_space=pl.ANY)
    k = ITERS
    dma = pltpu.SemaphoreType.DMA
    scratch = [
        pltpu.VMEM((rows, width), F32),
        pltpu.VMEM((rows, width), BF16),
        pltpu.VMEM((rows, width), BF16),
        pltpu.VMEM((rows, width), F32),
        pltpu.VMEM((k, group, depth), BF16),
        pltpu.VMEM((k, depth, group), BF16),
        pltpu.VMEM((k, S, NY, tokens, part), BF16),
        pltpu.VMEM((k, S, NY, tokens, part), BF16),
        pltpu.VMEM((k, S, NY, rows, part), BF16),
        pltpu.VMEM((k, S, depth, part), BF16),
        pltpu.VMEM((group, part), BF16),
        pltpu.VMEM((S, NY, rows, part), F32),
        pltpu.VMEM((k, S, NY, rows, part), BF16),
        pltpu.VMEM((k, S, NY, rows, part), BF16),
        pltpu.VMEM((k, S, NY, rows, part), BF16),
        pltpu.VMEM((k, S, NY, rows, part), BF16),
        pltpu.VMEM((k, S, rows, chunk // 2), BF16),
        pltpu.VMEM((k, S, rows, chunk // 2), BF16),
        dma((S + 2,)),
        dma((3, S)),
    ]
    for shape in ((k, 6), (k, S, 3), (k, S, 3), (k, S), (k, S), (k, S, 3), (k, S)):
        scratch += [dma(shape), dma(shape)]
    return pl.pallas_call(
        functools.partial(kernel, bits),
        out_shape=(
            jax.ShapeDtypeStruct(params.shape, F32),
            jax.ShapeDtypeStruct(moment.shape, BF16),
            jax.ShapeDtypeStruct(second.shape, BF16),
        ),
        in_specs=[anywhere] * 3 + [vmem] * 7,
        out_specs=(anywhere,) * 3,
        scratch_shapes=scratch,
        compiler_params=pltpu.CompilerParams(
            collective_id=collective_id, has_side_effects=True, vmem_limit_bytes=62 * 2**20
        ),
        cost_estimate=pl.CostEstimate(flops=2 * 10**10, bytes_accessed=2 * 10**7, transcendentals=0),
        name=f"window_{collective_id}",
    )(params, moment, second, active, target, ids, *tables)


def shards(params, moment, second, active, target, row_ids, step_index):
    levels = lax.axis_size("island").bit_length() - 1
    tables = [jnp.asarray(t) for t in cosine_tables()]
    branches = [
        functools.partial(window, tuple((b + k) % levels for k in range(ITERS)), b)
        for b in range(levels)
    ]
    out = lax.switch(
        jnp.remainder(step_index[0], levels),
        branches,
        params[0], moment[0], second[0], active[0], target[0], row_ids[:, 0, :], tables,
    )
    return tuple(o[None] for o in out)


def solution(mesh):
    in_specs = (
        P("island", "zero", None),
        P("island", "zero", None),
        P("island", "zero", None),
        P("island", "zero", None),
        P("island", "zero", None),
        P(None, "island", "zero"),
        P(),
    )
    out_specs = (P("island", "zero", None), P("island", "zero", None), P("island", "zero", None))
    return jax.shard_map(shards, mesh=mesh, in_specs=in_specs, out_specs=out_specs, check_vma=False)
```

```python
import functools
import math

import jax
import jax.numpy as jnp
import numpy as np
from jax import lax
from jax.experimental import pallas as pl
from jax.experimental.pallas import tpu as pltpu
from jax.sharding import PartitionSpec as P

MESH = pl.DeviceIdType.MESH
BF16 = jnp.bfloat16
F32 = jnp.float32

ITERS = 2
NY = 4
NX = 2
S = 4

beta_mean = 0.9
beta_square = 0.95
step_rate = 0.02
epsilon_add = 1e-08
gossip_rate = 0.4


def cosine_tables():
    places = np.arange(128)[:, None]
    orders = np.arange(64)[None, :]
    one = np.cos(math.pi * (places + 0.5) * orders / 128.0) * math.sqrt(2.0 / 128.0)
    one = np.where(orders == 0, one * math.sqrt(0.5), one)
    two = np.zeros((256, 128))
    two[:128, :64] = one
    two[128:, 64:] = one
    two = two.astype(np.float32)
    high = two.astype(jnp.bfloat16)
    low = (two - high.astype(np.float32)).astype(jnp.bfloat16)
    return high, low, np.ascontiguousarray(high.T), np.ascontiguousarray(low.T)


def dot(a, b):
    return jnp.dot(a, b, preferred_element_type=F32)


def kernel(
    bits,
    params_in, moment_in, second_in, act, tgt, ids, ch, cl, eh, el,
    params_out, moment_out, second_out,
    master, mean, square, left, x_all, x_turn, y_send, y_all, w_send, w_all,
    res, own, gx_send, gx_recv, gy_send, gy_recv, c_send, c_recv,
    in_sem, out_sem,
    xa_s, xa_r, ya_s, ya_r, wy_s, wy_r, wx_s, wx_r, gx_s, gx_r, gy_s, gy_r, c_s, c_r,
):
    rows, chunk = master.shape[1:]
    tokens = ids.shape[2]
    stored, depth = act.shape
    part = chunk // NY
    half = depth // NX
    island = lax.axis_index("island")
    z = lax.axis_index("zero")
    x = lax.rem(z, NX)
    y = lax.div(z, NX)
    other = 1 - x
    factor = 1.0 / math.sqrt(depth * tokens * NX * NY)

    def along_y(dy):
        return (island, lax.rem(y + dy, NY) * NX + x)

    across = (island, y * NX + other)
    partners = []
    for bit in bits:
        apart = 2**bit
        partners.append((island + apart * (1 - 2 * lax.rem(lax.div(island, apart), 2)), z))

    barrier = pltpu.get_barrier_semaphore()
    friends = [along_y(1), along_y(2), along_y(3), across] + partners
    for friend in friends:
        pl.semaphore_signal(barrier, inc=1, device_id=friend, device_id_type=MESH)

    def send(src, dst, s_sem, r_sem, device):
        pltpu.make_async_remote_copy(
            src_ref=src, dst_ref=dst, send_sem=s_sem, recv_sem=r_sem,
            device_id=device, device_id_type=MESH,
        ).start()

    def take(sem, like):
        pltpu.make_async_copy(like, like, sem).wait()

    def columns(s):
        return pl.ds(pl.multiple_of(s * chunk, chunk), chunk)

    for s in range(S):
        pltpu.make_async_copy(params_in.at[:, columns(s)], master.at[s], in_sem.at[s]).start()
    for s in range(S):
        pltpu.make_async_copy(moment_in.at[:, columns(s)], mean.at[s], in_sem.at[S]).start()
        pltpu.make_async_copy(second_in.at[:, columns(s)], square.at[s], in_sem.at[S + 1]).start()
    left[...] = jnp.zeros_like(left)

    def selector(k):
        spots = lax.broadcasted_iota(jnp.int32, (stored, tokens), 0)
        return jnp.where(spots == ids[k], 1.0, 0.0).astype(F32).T.astype(BF16)

    def pick_x(k):
        pick = selector(k)

        def step(b, _):
            block = dot(pick, act[:, pl.ds(pl.multiple_of(b * rows, rows), rows)])
            to = (lax.rem(b, NX) * NY + lax.div(b, NX)) * rows
            x_all[k, 0:tokens, pl.ds(pl.multiple_of(to, rows), rows)] = block.astype(BF16)
            return 0

        lax.fori_loop(0, NX * NY, step, 0, unroll=True)

    def pick_y(k):
        pick = selector(k)

        def step(s, _):
            block = dot(pick, tgt[:, columns(s)]).astype(BF16)
            for q in range(NY):
                y_send[k, s, q] = block[:, q * part : (q + 1) * part]
            return 0

        lax.fori_loop(0, S, step, 0, unroll=True)

    def turn(k, slot):
        def step(b, _):
            at = pl.multiple_of(b * rows, rows)
            block = x_all[k, slot * tokens : (slot + 1) * tokens, pl.ds(at, rows)]
            x_turn[k, pl.ds(at, rows), slot * tokens : (slot + 1) * tokens] = block.T
            return 0

        lax.fori_loop(0, depth // rows, step, 0, unroll=True)

    def x_rows(k, slot, which):
        return x_all.at[k, pl.ds(slot * tokens + which * (tokens // 2), tokens // 2)]

    def x_first(k):
        for n, (which, dy, slot) in enumerate(((0, 1, 1), (1, 3, 2), (1, 1, 1), (0, 3, 2))):
            send(x_rows(k, 0, which), x_rows(k, slot, which), xa_s, xa_r.at[k, min(n, 2)], along_y(dy))

    def x_second(k):
        take(xa_r.at[k, 0], x_rows(k, 1, 0))
        send(x_rows(k, 1, 0), x_rows(k, 3, 0), xa_s, xa_r.at[k, 3], along_y(1))
        take(xa_r.at[k, 1], x_rows(k, 2, 1))
        send(x_rows(k, 2, 1), x_rows(k, 3, 1), xa_s, xa_r.at[k, 3], along_y(3))

    def x_last(k):
        both = x_all.at[k, pl.ds(0, tokens)]
        take(xa_r.at[k, 2], both)
        turn(k, 1)
        turn(k, 2)
        take(xa_r.at[k, 3], both)
        turn(k, 3)

    slot_of = {1: 1, 3: 2, 2: 3}

    def y_first(k, s):
        for dy in (1, 3, 2):
            send(
                y_send.at[k, s, lax.rem(y + dy, NY)], y_all.at[k, s, slot_of[dy]],
                ya_s, ya_r.at[k, s], along_y(dy),
            )
        y_all[k, s, 0] = y_send[k, s, y]

    def w_first(k, s):
        for q in range(NY):
            w_send[k, s, q] = master[s, :, q * part : (q + 1) * part].astype(BF16)
        mine = pl.ds(pl.multiple_of((x * NY + y) * rows, rows), rows)
        for dy in (1, 3, 2):
            send(
                w_send.at[k, s, lax.rem(y + dy, NY)], w_all.at[k, s, mine],
                wy_s, wy_r.at[s], along_y(dy),
            )
        w_all[k, s, mine] = w_send[k, s, y]

    def w_second(k, s):
        take(wy_r.at[s], w_send.at[k, s, pl.ds(0, NY - 1)])
        mine = w_all.at[k, s, pl.ds(pl.multiple_of(x * half, half), half)]
        send(mine, mine, wx_s, wx_r.at[s], across)

    def work(k, s):
        @pl.when(s == 0)
        def _():
            x_last(k)

        take(ya_r.at[k, s], y_send.at[k, s, pl.ds(0, NY - 1)])
        take(wx_r.at[s], gx_send.at[k, s])

        def residual(slot, _):
            at = pl.ds(pl.multiple_of(slot * tokens, tokens), tokens)
            out = dot(x_all[k, at, :], w_all[k, s])
            res[at, :] = (out - y_all[k, s, slot].astype(F32)).astype(BF16)
            return 0

        lax.fori_loop(0, NY, residual, 0, unroll=True)

        def term(side, b):
            at = pl.multiple_of(side * half + b * rows, rows)
            return dot(x_turn[k, pl.ds(at, rows), :], res[...])

        def theirs(b, _):
            gx_send[k, s, b] = term(other, b).astype(BF16)
            return 0

        def ours(b, _):
            own[s, b] = term(x, b)
            return 0

        lax.fori_loop(0, NY, theirs, 0, unroll=True)
        send(gx_send.at[k, s], gx_recv.at[k, s], gx_s, gx_r.at[s], across)
        lax.fori_loop(0, NY, ours, 0, unroll=True)

    def add(k, s):
        take(gx_r.at[s], gx_recv.at[k, s])
        for b in range(NY):
            gy_send[k, s, b] = (own[s, b] + gx_recv[k, s, b].astype(F32)).astype(BF16)
        for dy in (1, 3, 2):
            send(
                gy_send.at[k, s, lax.rem(y + dy, NY)], gy_recv.at[k, s, y],
                gy_s, gy_r.at[s], along_y(dy),
            )
        gy_recv[k, s, y] = gy_send[k, s, y]

    def expand(c):
        return dot(c, eh[...]) + dot(c, el[...])

    wide = 256

    def update(k, s):
        take(gy_r.at[s], gy_send.at[k, s, pl.ds(0, NY - 1)])

        @pl.when(jnp.logical_and(k == 0, s == 0))
        def _():
            take(in_sem.at[S], mean)
            take(in_sem.at[S + 1], square)

        for j in range(chunk // wide):
            cols = slice(j * wide, (j + 1) * wide)
            per = wide // part
            grad = jnp.concatenate([gy_recv[k, s, j * per + q] for q in range(per)], axis=1)
            grad = grad.astype(F32) * factor
            mean_next = beta_mean * mean[s, :, cols].astype(F32) + (1.0 - beta_mean) * grad
            square_next = beta_square * square[s, :, cols].astype(F32) + (1.0 - beta_square) * grad * grad
            mean[s, :, cols] = mean_next.astype(BF16)
            square[s, :, cols] = square_next.astype(BF16)
            updated = master[s, :, cols] - step_rate * mean_next / (jnp.sqrt(square_next) + epsilon_add)
            carried = updated + left[s, :, cols]
            high = carried.astype(BF16)
            low = (carried - high.astype(F32)).astype(BF16)
            coeffs = (dot(high, ch[...]) + (dot(low, ch[...]) + dot(high, cl[...]))).astype(BF16)
            c_send[k, s, :, j * (wide // 2) : (j + 1) * (wide // 2)] = coeffs
            back = expand(coeffs)
            left[s, :, cols] = carried - back
            master[s, :, cols] = updated - gossip_rate * back
        partner = (partners[0][0] + k * (partners[1][0] - partners[0][0]), z)
        send(c_send.at[k, s], c_recv.at[k, s], c_s, c_r.at[k, s], partner)

        @pl.when(k + 1 == ITERS)
        def _():
            pltpu.make_async_copy(mean.at[s], moment_out.at[:, columns(s)], out_sem.at[1]).start()
            pltpu.make_async_copy(square.at[s], second_out.at[:, columns(s)], out_sem.at[2]).start()

    def gossip(k, s):
        take(c_r.at[k, s], c_recv.at[k, s])
        remote = c_recv[k, s]
        for j in range(chunk // wide):
            cols = slice(j * wide, (j + 1) * wide)
            piece = remote[:, j * (wide // 2) : (j + 1) * (wide // 2)]
            master[s, :, cols] = master[s, :, cols] + gossip_rate * expand(piece)

        @pl.when(k + 1 == ITERS)
        def _():
            pltpu.make_async_copy(master.at[s], params_out.at[:, columns(s)], out_sem.at[0]).start()

        @pl.when(k + 1 < ITERS)
        def _():
            w_first(k + 1, s)

    pick_x(0)
    take(in_sem.at[0], master.at[0])
    pl.semaphore_wait(barrier, len(friends))
    w_first(0, 0)
    x_first(0)
    pick_y(0)
    y_first(0, 0)
    turn(0, 0)
    x_second(0)

    def more(s, _):
        take(in_sem.at[s], master.at[s])
        w_first(0, s)
        y_first(0, s)
        return 0

    lax.fori_loop(1, S, more, 0)
    pick_x(1)
    pick_y(1)
    turn(1, 0)

    stages = [w_second, work, add, update, gossip]
    count = len(stages) * ITERS

    def slot(t, _):
        @pl.when(t == 2)
        def _():
            x_first(1)

        @pl.when(t == 4)
        def _():
            x_second(1)
            lax.fori_loop(0, S, lambda s, _: (y_first(1, s), 0)[1], 0)

        def visit(s, _):
            at = t - s
            for n, stage in enumerate(stages):
                @pl.when(jnp.logical_and(jnp.logical_and(at >= 0, at < count), lax.rem(at, len(stages)) == n))
                def _(stage=stage):
                    stage(lax.div(at, len(stages)), s)

            return 0

        lax.fori_loop(0, S, visit, 0)
        return 0

    lax.fori_loop(0, count + S - 1, slot, 0)

    take(xa_s, x_all.at[:, pl.ds(0, 3 * tokens)])
    take(ya_s, y_send.at[:, :, pl.ds(0, NY - 1)])
    take(wy_s, w_send.at[:, :, pl.ds(0, NY - 1)])
    take(wx_s, gx_send)
    take(gx_s, gx_send)
    take(gy_s, gy_send.at[:, :, pl.ds(0, NY - 1)])
    take(c_s, c_recv)
    take(out_sem.at[0], master)
    take(out_sem.at[1], mean)
    take(out_sem.at[2], square)


def window(bits, cid, params, moment, second, active, target, ids, tables):
    rows, width = params.shape
    depth = active.shape[1]
    tokens = ids.shape[2]
    chunk = width // S
    part = chunk // NY
    group = tokens * NY
    vmem = pl.BlockSpec(memory_space=pltpu.VMEM)
    anywhere = pl.BlockSpec(memory_space=pl.ANY)
    k = ITERS
    dma = pltpu.SemaphoreType.DMA
    scratch = [
        pltpu.VMEM((S, rows, chunk), F32),
        pltpu.VMEM((S, rows, chunk), BF16),
        pltpu.VMEM((S, rows, chunk), BF16),
        pltpu.VMEM((S, rows, chunk), F32),
        pltpu.VMEM((k, group, depth), BF16),
        pltpu.VMEM((k, depth, group), BF16),
        pltpu.VMEM((k, S, NY, tokens, part), BF16),
        pltpu.VMEM((k, S, NY, tokens, part), BF16),
        pltpu.VMEM((k, S, NY, rows, part), BF16),
        pltpu.VMEM((k, S, depth, part), BF16),
        pltpu.VMEM((group, part), BF16),
        pltpu.VMEM((S, NY, rows, part), F32),
        pltpu.VMEM((k, S, NY, rows, part), BF16),
        pltpu.VMEM((k, S, NY, rows, part), BF16),
        pltpu.VMEM((k, S, NY, rows, part), BF16),
        pltpu.VMEM((k, S, NY, rows, part), BF16),
        pltpu.VMEM((k, S, rows, chunk // 2), BF16),
        pltpu.VMEM((k, S, rows, chunk // 2), BF16),
        dma((S + 2,)),
        dma((3,)),
    ]
    for shape in ((k, 4), (k, S), (S,), (S,), (S,), (S,), (k, S)):
        scratch += [dma, dma(shape)]
    return pl.pallas_call(
        functools.partial(kernel, bits),
        out_shape=(
            jax.ShapeDtypeStruct(params.shape, F32),
            jax.ShapeDtypeStruct(moment.shape, BF16),
            jax.ShapeDtypeStruct(second.shape, BF16),
        ),
        in_specs=[anywhere] * 3 + [vmem] * 3 + [vmem] * 4,
        out_specs=(anywhere,) * 3,
        scratch_shapes=scratch,
        compiler_params=pltpu.CompilerParams(
            collective_id=cid, has_side_effects=True, vmem_limit_bytes=62 * 2**20
        ),
        cost_estimate=pl.CostEstimate(flops=2 * 10**10, bytes_accessed=2 * 10**7, transcendentals=0),
        name=f"window_{cid}",
    )(params, moment, second, active, target, ids, *tables)


def shards(params, moment, second, active, target, row_ids, step_index):
    levels = lax.axis_size("island").bit_length() - 1
    tables = [jnp.asarray(t) for t in cosine_tables()]
    branches = [
        functools.partial(window, tuple((b + k) % levels for k in range(ITERS)), b)
        for b in range(levels)
    ]
    out = lax.switch(
        jnp.remainder(step_index[0], levels),
        branches,
        params[0], moment[0], second[0], active[0], target[0], row_ids, tables,
    )
    return tuple(o[None] for o in out)


def solution(mesh):
    in_specs = (
        P("island", "zero", None),
        P("island", "zero", None),
        P("island", "zero", None),
        P("island", "zero", None),
        P("island", "zero", None),
        P(None, "island", "zero"),
        P(),
    )
    out_specs = (P("island", "zero", None), P("island", "zero", None), P("island", "zero", None))
    return jax.shard_map(shards, mesh=mesh, in_specs=in_specs, out_specs=out_specs, check_vma=False)
```

```python
import functools
import math

import jax
import jax.numpy as jnp
import numpy as np
from jax import lax
from jax.experimental import pallas as pl
from jax.experimental.pallas import tpu as pltpu
from jax.sharding import PartitionSpec as P

MESH = pl.DeviceIdType.MESH
BF16 = jnp.bfloat16
F32 = jnp.float32

ITERS = 2
NY = 4
NX = 2
S = 4

beta_mean = 0.9
beta_square = 0.95
step_rate = 0.02
epsilon_add = 1e-08
gossip_rate = 0.4


def cosine_tables():
    places = np.arange(128)[:, None]
    orders = np.arange(64)[None, :]
    one = np.cos(math.pi * (places + 0.5) * orders / 128.0) * math.sqrt(2.0 / 128.0)
    one = np.where(orders == 0, one * math.sqrt(0.5), one)
    two = np.zeros((256, 128))
    two[:128, :64] = one
    two[128:, 64:] = one
    two = two.astype(np.float32)
    high = two.astype(jnp.bfloat16)
    low = (two - high.astype(np.float32)).astype(jnp.bfloat16)
    return high, low, np.concatenate([high.T, low.T])


def dot(a, b):
    return jnp.dot(a, b, preferred_element_type=F32)


def kernel(
    bits,
    params_in, moment_in, second_in, act_in, tgt_in, ids, ch, cl, e,
    params_out, moment_out, second_out,
    act, tgt, master, mean, square, left, x_all, x_turn, y_send, y_all, w_send, w_all,
    res, own, gx_send, gx_recv, gy_send, gy_recv, c_send, c_recv,
    in_sem, out_sem,
    xa_s, xa_r, ya_s, ya_r, wy_s, wy_r, wx_s, wx_r, gx_s, gx_r, gy_s, gy_r, c_s, c_r,
):
    rows, chunk = master.shape[1:]
    tokens = ids.shape[2]
    stored, depth = act.shape
    part = chunk // NY
    half = depth // NX
    island = lax.axis_index("island")
    z = lax.axis_index("zero")
    x = lax.rem(z, NX)
    y = lax.div(z, NX)
    other = 1 - x
    factor = 1.0 / math.sqrt(depth * tokens * NX * NY)

    def along_y(dy):
        return (island, lax.rem(y + dy, NY) * NX + x)

    across = (island, y * NX + other)
    partners = []
    for bit in bits:
        apart = 2**bit
        partners.append((island + apart * (1 - 2 * lax.rem(lax.div(island, apart), 2)), z))

    barrier = pltpu.get_barrier_semaphore()
    friends = [along_y(1), along_y(2), along_y(3), across] + partners
    for friend in friends:
        pl.semaphore_signal(barrier, inc=1, device_id=friend, device_id_type=MESH)

    def send(src, dst, s_sem, r_sem, device):
        pltpu.make_async_remote_copy(
            src_ref=src, dst_ref=dst, send_sem=s_sem, recv_sem=r_sem,
            device_id=device, device_id_type=MESH,
        ).start()

    def take(sem, like):
        pltpu.make_async_copy(like, like, sem).wait()

    def columns(s):
        return pl.ds(pl.multiple_of(s * chunk, chunk), chunk)

    pltpu.make_async_copy(act_in, act, in_sem.at[S + 2]).start()
    for s in range(S):
        pltpu.make_async_copy(params_in.at[:, columns(s)], master.at[s], in_sem.at[s]).start()
    for s in range(S):
        pltpu.make_async_copy(moment_in.at[:, columns(s)], mean.at[s], in_sem.at[S]).start()
        pltpu.make_async_copy(second_in.at[:, columns(s)], square.at[s], in_sem.at[S + 1]).start()
    pltpu.make_async_copy(tgt_in, tgt, in_sem.at[S + 3]).start()
    left[...] = jnp.zeros_like(left)

    def selector(k):
        spots = lax.broadcasted_iota(jnp.int32, (stored, tokens), 0)
        return jnp.where(spots == ids[k], 1.0, 0.0).astype(F32).T.astype(BF16)

    def pick_x(k):
        pick = selector(k)

        def step(b, _):
            block = dot(pick, act[:, pl.ds(pl.multiple_of(b * rows, rows), rows)])
            to = (lax.rem(b, NX) * NY + lax.div(b, NX)) * rows
            x_all[k, 0:tokens, pl.ds(pl.multiple_of(to, rows), rows)] = block.astype(BF16)
            return 0

        lax.fori_loop(0, NX * NY, step, 0, unroll=True)

    def pick_y(k):
        pick = selector(k)

        def step(s, _):
            block = dot(pick, tgt[:, columns(s)]).astype(BF16)
            for q in range(NY):
                y_send[k, s, q] = block[:, q * part : (q + 1) * part]
            return 0

        lax.fori_loop(0, S, step, 0, unroll=True)

    def turn(k, slot):
        def step(b, _):
            at = pl.multiple_of(b * rows, rows)
            block = x_all[k, slot * tokens : (slot + 1) * tokens, pl.ds(at, rows)]
            x_turn[k, pl.ds(at, rows), slot * tokens : (slot + 1) * tokens] = block.T
            return 0

        lax.fori_loop(0, depth // rows, step, 0, unroll=True)

    def x_rows(k, slot, which):
        return x_all.at[k, pl.ds(slot * tokens + which * (tokens // 2), tokens // 2)]

    def x_first(k):
        for n, (which, dy, slot) in enumerate(((0, 1, 1), (1, 3, 2), (1, 1, 1), (0, 3, 2))):
            send(x_rows(k, 0, which), x_rows(k, slot, which), xa_s, xa_r.at[k, min(n, 2)], along_y(dy))

    def x_second(k):
        take(xa_r.at[k, 0], x_rows(k, 1, 0))
        send(x_rows(k, 1, 0), x_rows(k, 3, 0), xa_s, xa_r.at[k, 3], along_y(1))
        take(xa_r.at[k, 1], x_rows(k, 2, 1))
        send(x_rows(k, 2, 1), x_rows(k, 3, 1), xa_s, xa_r.at[k, 3], along_y(3))

    def x_last(k):
        both = x_all.at[k, pl.ds(0, tokens)]
        take(xa_r.at[k, 2], both)
        turn(k, 1)
        turn(k, 2)
        take(xa_r.at[k, 3], both)
        turn(k, 3)

    slot_of = {1: 1, 3: 2, 2: 3}

    def y_first(k, s):
        for dy in (1, 3, 2):
            send(
                y_send.at[k, s, lax.rem(y + dy, NY)], y_all.at[k, s, slot_of[dy]],
                ya_s, ya_r.at[k, s], along_y(dy),
            )
        y_all[k, s, 0] = y_send[k, s, y]

    def w_first(k, s):
        for q in range(NY):
            w_send[k, s, q] = master[s, :, q * part : (q + 1) * part].astype(BF16)
        mine = pl.ds(pl.multiple_of((x * NY + y) * rows, rows), rows)
        for dy in (1, 3, 2):
            send(
                w_send.at[k, s, lax.rem(y + dy, NY)], w_all.at[k, s, mine],
                wy_s, wy_r.at[s], along_y(dy),
            )
        w_all[k, s, mine] = w_send[k, s, y]

    def w_second(k, s):
        take(wy_r.at[s], w_send.at[k, s, pl.ds(0, NY - 1)])
        mine = w_all.at[k, s, pl.ds(pl.multiple_of(x * half, half), half)]
        send(mine, mine, wx_s, wx_r.at[s], across)

    def work(k, s):
        @pl.when(s == 0)
        def _():
            x_last(k)

        take(ya_r.at[k, s], y_send.at[k, s, pl.ds(0, NY - 1)])
        take(wx_r.at[s], gx_send.at[k, s])

        def residual(slot, _):
            at = pl.ds(pl.multiple_of(slot * tokens, tokens), tokens)
            out = dot(x_all[k, at, :], w_all[k, s])
            res[at, :] = (out - y_all[k, s, slot].astype(F32)).astype(BF16)
            return 0

        lax.fori_loop(0, NY, residual, 0, unroll=True)

        def term(side, b):
            at = pl.multiple_of(side * half + b * rows, rows)
            return dot(x_turn[k, pl.ds(at, rows), :], res[...])

        def theirs(b, _):
            gx_send[k, s, b] = term(other, b).astype(BF16)
            return 0

        def ours(b, _):
            own[s, b] = term(x, b)
            return 0

        lax.fori_loop(0, NY, theirs, 0, unroll=True)
        send(gx_send.at[k, s], gx_recv.at[k, s], gx_s, gx_r.at[s], across)
        lax.fori_loop(0, NY, ours, 0, unroll=True)

    def add(k, s):
        take(gx_r.at[s], gx_recv.at[k, s])
        for b in range(NY):
            gy_send[k, s, b] = (own[s, b] + gx_recv[k, s, b].astype(F32)).astype(BF16)
        for dy in (1, 3, 2):
            send(
                gy_send.at[k, s, lax.rem(y + dy, NY)], gy_recv.at[k, s, y],
                gy_s, gy_r.at[s], along_y(dy),
            )
        gy_recv[k, s, y] = gy_send[k, s, y]

    def expand(c):
        return dot(jnp.concatenate([c, c], axis=1), e[...])

    wide = 256

    def update(k, s):
        take(gy_r.at[s], gy_send.at[k, s, pl.ds(0, NY - 1)])

        @pl.when(jnp.logical_and(k == 0, s == 0))
        def _():
            take(in_sem.at[S], mean)
            take(in_sem.at[S + 1], square)

        for j in range(chunk // wide):
            cols = slice(j * wide, (j + 1) * wide)
            per = wide // part
            grad = jnp.concatenate([gy_recv[k, s, j * per + q] for q in range(per)], axis=1)
            grad = grad.astype(F32) * factor
            mean_next = beta_mean * mean[s, :, cols].astype(F32) + (1.0 - beta_mean) * grad
            square_next = beta_square * square[s, :, cols].astype(F32) + (1.0 - beta_square) * grad * grad
            mean[s, :, cols] = mean_next.astype(BF16)
            square[s, :, cols] = square_next.astype(BF16)
            updated = master[s, :, cols] - step_rate * mean_next / (jnp.sqrt(square_next) + epsilon_add)
            carried = updated + left[s, :, cols]
            high = carried.astype(BF16)
            low = (carried - high.astype(F32)).astype(BF16)
            coeffs = (dot(high, ch[...]) + (dot(low, ch[...]) + dot(high, cl[...]))).astype(BF16)
            c_send[k, s, :, j * (wide // 2) : (j + 1) * (wide // 2)] = coeffs
            back = expand(coeffs)
            left[s, :, cols] = carried - back
            master[s, :, cols] = updated - gossip_rate * back
        partner = (partners[0][0] + k * (partners[1][0] - partners[0][0]), z)
        send(c_send.at[k, s], c_recv.at[k, s], c_s, c_r.at[k, s], partner)

        @pl.when(k + 1 == ITERS)
        def _():
            pltpu.make_async_copy(mean.at[s], moment_out.at[:, columns(s)], out_sem.at[1]).start()
            pltpu.make_async_copy(square.at[s], second_out.at[:, columns(s)], out_sem.at[2]).start()

    def gossip(k, s):
        take(c_r.at[k, s], c_recv.at[k, s])
        remote = c_recv[k, s]
        for j in range(chunk // wide):
            cols = slice(j * wide, (j + 1) * wide)
            piece = remote[:, j * (wide // 2) : (j + 1) * (wide // 2)]
            master[s, :, cols] = master[s, :, cols] + gossip_rate * expand(piece)

        @pl.when(k + 1 == ITERS)
        def _():
            pltpu.make_async_copy(master.at[s], params_out.at[:, columns(s)], out_sem.at[0]).start()

        @pl.when(k + 1 < ITERS)
        def _():
            w_first(k + 1, s)

    take(in_sem.at[S + 2], act)
    pick_x(0)
    take(in_sem.at[0], master.at[0])
    pl.semaphore_wait(barrier, len(friends))
    w_first(0, 0)
    x_first(0)
    take(in_sem.at[S + 3], tgt)
    pick_y(0)
    y_first(0, 0)
    turn(0, 0)
    x_second(0)

    def more(s, _):
        take(in_sem.at[s], master.at[s])
        w_first(0, s)
        y_first(0, s)
        return 0

    lax.fori_loop(1, S, more, 0)
    pick_x(1)
    pick_y(1)
    turn(1, 0)

    stages = [w_second, work, add, update, gossip]
    count = len(stages) * ITERS

    def slot(t, _):
        @pl.when(t == 2)
        def _():
            x_first(1)

        @pl.when(t == 4)
        def _():
            x_second(1)
            lax.fori_loop(0, S, lambda s, _: (y_first(1, s), 0)[1], 0)

        def visit(r, _):
            s = S - 1 - r
            at = t - s
            for n, stage in enumerate(stages):
                @pl.when(jnp.logical_and(jnp.logical_and(at >= 0, at < count), lax.rem(at, len(stages)) == n))
                def _(stage=stage):
                    stage(lax.div(at, len(stages)), s)

            return 0

        lax.fori_loop(0, S, visit, 0)
        return 0

    lax.fori_loop(0, count + S - 1, slot, 0)

    take(xa_s, x_all.at[:, pl.ds(0, 3 * tokens)])
    take(ya_s, y_send.at[:, :, pl.ds(0, NY - 1)])
    take(wy_s, w_send.at[:, :, pl.ds(0, NY - 1)])
    take(wx_s, gx_send)
    take(gx_s, gx_send)
    take(gy_s, gy_send.at[:, :, pl.ds(0, NY - 1)])
    take(c_s, c_recv)
    take(out_sem.at[0], master)
    take(out_sem.at[1], mean)
    take(out_sem.at[2], square)


def window(bits, cid, params, moment, second, active, target, ids, tables):
    rows, width = params.shape
    depth = active.shape[1]
    tokens = ids.shape[2]
    chunk = width // S
    part = chunk // NY
    group = tokens * NY
    vmem = pl.BlockSpec(memory_space=pltpu.VMEM)
    anywhere = pl.BlockSpec(memory_space=pl.ANY)
    k = ITERS
    dma = pltpu.SemaphoreType.DMA
    scratch = [
        pltpu.VMEM(active.shape, BF16),
        pltpu.VMEM(target.shape, BF16),
        pltpu.VMEM((S, rows, chunk), F32),
        pltpu.VMEM((S, rows, chunk), BF16),
        pltpu.VMEM((S, rows, chunk), BF16),
        pltpu.VMEM((S, rows, chunk), F32),
        pltpu.VMEM((k, group, depth), BF16),
        pltpu.VMEM((k, depth, group), BF16),
        pltpu.VMEM((k, S, NY, tokens, part), BF16),
        pltpu.VMEM((k, S, NY, tokens, part), BF16),
        pltpu.VMEM((k, S, NY, rows, part), BF16),
        pltpu.VMEM((k, S, depth, part), BF16),
        pltpu.VMEM((group, part), BF16),
        pltpu.VMEM((S, NY, rows, part), F32),
        pltpu.VMEM((k, S, NY, rows, part), BF16),
        pltpu.VMEM((k, S, NY, rows, part), BF16),
        pltpu.VMEM((k, S, NY, rows, part), BF16),
        pltpu.VMEM((k, S, NY, rows, part), BF16),
        pltpu.VMEM((k, S, rows, chunk // 2), BF16),
        pltpu.VMEM((k, S, rows, chunk // 2), BF16),
        dma((S + 4,)),
        dma((3,)),
    ]
    for shape in ((k, 4), (k, S), (S,), (S,), (S,), (S,), (k, S)):
        scratch += [dma, dma(shape)]
    return pl.pallas_call(
        functools.partial(kernel, bits),
        out_shape=(
            pltpu.VMEM(params.shape, F32),
            pltpu.VMEM(moment.shape, BF16),
            pltpu.VMEM(second.shape, BF16),
        ),
        in_specs=[anywhere] * 5 + [vmem] * 4,
        out_specs=(vmem,) * 3,
        scratch_shapes=scratch,
        compiler_params=pltpu.CompilerParams(
            collective_id=cid, has_side_effects=True, vmem_limit_bytes=54 * 2**20
        ),
        cost_estimate=pl.CostEstimate(flops=2 * 10**10, bytes_accessed=2 * 10**7, transcendentals=0),
        name=f"window_{cid}",
    )(params, moment, second, active, target, ids, *tables)


def shards(params, moment, second, active, target, row_ids, step_index):
    levels = lax.axis_size("island").bit_length() - 1
    tables = [jnp.asarray(t) for t in cosine_tables()]
    branches = [
        functools.partial(window, tuple((b + k) % levels for k in range(ITERS)), b)
        for b in range(levels)
    ]
    out = lax.switch(
        jnp.remainder(step_index[0], levels),
        branches,
        params[0], moment[0], second[0], active[0], target[0], row_ids, tables,
    )
    return tuple(o[None] for o in out)


def solution(mesh):
    in_specs = (
        P("island", "zero", None),
        P("island", "zero", None),
        P("island", "zero", None),
        P("island", "zero", None),
        P("island", "zero", None),
        P(None, "island", "zero"),
        P(),
    )
    out_specs = (P("island", "zero", None), P("island", "zero", None), P("island", "zero", None))
    return jax.shard_map(shards, mesh=mesh, in_specs=in_specs, out_specs=out_specs, check_vma=False)
```

```python
import functools
import math

import jax
import jax.numpy as jnp
import numpy as np
from jax import lax
from jax.experimental import pallas as pl
from jax.experimental.pallas import tpu as pltpu
from jax.sharding import PartitionSpec as P

MESH = pl.DeviceIdType.MESH
BF16 = jnp.bfloat16
F32 = jnp.float32

ITERS = 2
NY = 4
NX = 2
S = 4

beta_mean = 0.9
beta_square = 0.95
step_rate = 0.02
epsilon_add = 1e-08
gossip_rate = 0.4


def cosine_tables():
    places = np.arange(128)[:, None]
    orders = np.arange(64)[None, :]
    one = np.cos(math.pi * (places + 0.5) * orders / 128.0) * math.sqrt(2.0 / 128.0)
    one = np.where(orders == 0, one * math.sqrt(0.5), one)
    two = np.zeros((256, 128))
    two[:128, :64] = one
    two[128:, 64:] = one
    two = two.astype(np.float32)
    high = two.astype(jnp.bfloat16)
    low = (two - high.astype(np.float32)).astype(jnp.bfloat16)
    return high, low, np.concatenate([high.T, low.T])


def dot(a, b):
    return jnp.dot(a, b, preferred_element_type=F32)


def kernel(
    bits,
    params_in, moment_in, second_in, act_in, tgt_in, ids, ch, cl, e,
    params_out, moment_out, second_out,
    act, tgt, master, mean, square, left, x_all, x_turn, y_send, y_all, w_send, w_all,
    res, own, gx_send, gx_recv, gy_send, gy_recv, c_send, c_recv,
    in_sem, out_sem,
    xa_s, xa_r, ya_s, ya_r, wy_s, wy_r, wx_s, wx_r, gx_s, gx_r, gy_s, gy_r, c_s, c_r,
):
    rows, chunk = master.shape[1:]
    tokens = ids.shape[2]
    stored, depth = act.shape
    part = chunk // NY
    half = depth // NX
    island = lax.axis_index("island")
    z = lax.axis_index("zero")
    factor = 1.0 / math.sqrt(depth * tokens * NX * NY)

    core = lax.rem(island, 2)
    bit_x = lax.rem(z, 2)
    bit_b = lax.div(z, 4)
    bit_a = lax.rem(lax.rem(lax.div(z, 2), 2) + bit_b, 2)
    u = bit_a
    v = bit_b * (1 - core) + bit_x * core
    side = bit_x * (1 - core) + bit_b * core
    spot = 2 * u + v
    other = 1 - side

    def across_edges(a, b, x):
        to_a, to_b, to_x = lax.rem(bit_a + a, 2), lax.rem(bit_b + b, 2), lax.rem(bit_x + x, 2)
        return (island, 4 * to_b + 2 * lax.rem(to_a + to_b, 2) + to_x)

    peers = [
        (across_edges(1, 0, 0), 2 * (1 - u) + v),
        (across_edges(0, 1 - core, core), 2 * u + (1 - v)),
        (across_edges(1, 1 - core, core), 2 * (1 - u) + (1 - v)),
    ]
    across = across_edges(0, core, 1 - core)

    def position(block):
        x = lax.rem(block, 2)
        b = lax.div(block, 4)
        a = lax.rem(lax.rem(lax.div(block, 2), 2) + b, 2)
        return (x * (1 - core) + b * core) * NY + 2 * a + b * (1 - core) + x * core

    partners = []
    for bit in bits:
        apart = 2**bit
        partners.append((island + apart * (1 - 2 * lax.rem(lax.div(island, apart), 2)), z))

    barrier = pltpu.get_barrier_semaphore()
    friends = [device for device, _ in peers] + [across] + partners
    for friend in friends:
        pl.semaphore_signal(barrier, inc=1, device_id=friend, device_id_type=MESH)

    def send(src, dst, s_sem, r_sem, device):
        pltpu.make_async_remote_copy(
            src_ref=src, dst_ref=dst, send_sem=s_sem, recv_sem=r_sem,
            device_id=device, device_id_type=MESH,
        ).start()

    def take(sem, like):
        pltpu.make_async_copy(like, like, sem).wait()

    def columns(s):
        return pl.ds(pl.multiple_of(s * chunk, chunk), chunk)

    pltpu.make_async_copy(act_in, act, in_sem.at[S + 2]).start()
    for s in range(S):
        pltpu.make_async_copy(params_in.at[:, columns(s)], master.at[s], in_sem.at[s]).start()
    for s in range(S):
        pltpu.make_async_copy(moment_in.at[:, columns(s)], mean.at[s], in_sem.at[S]).start()
        pltpu.make_async_copy(second_in.at[:, columns(s)], square.at[s], in_sem.at[S + 1]).start()
    pltpu.make_async_copy(tgt_in, tgt, in_sem.at[S + 3]).start()
    left[...] = jnp.zeros_like(left)

    def selector(k):
        spots = lax.broadcasted_iota(jnp.int32, (stored, tokens), 0)
        return jnp.where(spots == ids[k], 1.0, 0.0).astype(F32).T.astype(BF16)

    def pick_x(k):
        pick = selector(k)

        def step(b, _):
            block = dot(pick, act[:, pl.ds(pl.multiple_of(b * rows, rows), rows)])
            to = position(b) * rows
            x_all[k, 0:tokens, pl.ds(pl.multiple_of(to, rows), rows)] = block.astype(BF16)
            return 0

        lax.fori_loop(0, NX * NY, step, 0, unroll=True)

    def pick_y(k):
        pick = selector(k)

        def step(s, _):
            block = dot(pick, tgt[:, columns(s)]).astype(BF16)
            for q in range(NY):
                y_send[k, s, q] = block[:, q * part : (q + 1) * part]
            return 0

        lax.fori_loop(0, S, step, 0, unroll=True)

    def turn(k, slot):
        def step(b, _):
            at = pl.multiple_of(b * rows, rows)
            block = x_all[k, slot * tokens : (slot + 1) * tokens, pl.ds(at, rows)]
            x_turn[k, pl.ds(at, rows), slot * tokens : (slot + 1) * tokens] = block.T
            return 0

        lax.fori_loop(0, depth // rows, step, 0, unroll=True)

    def x_rows(k, slot, which):
        return x_all.at[k, pl.ds(slot * tokens + which * (tokens // 2), tokens // 2)]

    def x_first(k):
        mine = x_all.at[k, pl.ds(0, tokens)]
        for which in range(2):
            send(x_rows(k, 0, which), x_rows(k, 1, which), xa_s, xa_r.at[k, which], peers[0][0])
        send(mine, x_all.at[k, pl.ds(2 * tokens, tokens)], xa_s, xa_r.at[k, 2], peers[1][0])

    def x_second(k, which):
        take(xa_r.at[k, which], x_rows(k, 1, which))
        send(x_rows(k, 1, which), x_rows(k, 3, which), xa_s, xa_r.at[k, 3], peers[1][0])

    def x_last(k):
        turn(k, 1)
        take(xa_r.at[k, 2], x_all.at[k, pl.ds(0, tokens)])
        turn(k, 2)
        take(xa_r.at[k, 3], x_all.at[k, pl.ds(0, tokens)])
        turn(k, 3)

    def y_first(k, s):
        for n, (device, place) in enumerate(peers):
            send(y_send.at[k, s, place], y_all.at[k, s, n + 1], ya_s, ya_r.at[k, s], device)
        y_all[k, s, 0] = y_send[k, s, spot]

    def w_first(k, s):
        for q in range(NY):
            w_send[k, s, q] = master[s, :, q * part : (q + 1) * part].astype(BF16)
        mine = pl.ds(pl.multiple_of((side * NY + spot) * rows, rows), rows)
        for device, place in peers:
            send(w_send.at[k, s, place], w_all.at[k, s, mine], wy_s, wy_r.at[s], device)
        w_all[k, s, mine] = w_send[k, s, spot]

    def w_second(k, s):
        take(wy_r.at[s], w_send.at[k, s, pl.ds(0, NY - 1)])
        mine = w_all.at[k, s, pl.ds(pl.multiple_of(side * half, half), half)]
        send(mine, mine, wx_s, wx_r.at[s], across)

    def work(k, s):
        @pl.when(s == 0)
        def _():
            x_last(k)

        take(ya_r.at[k, s], y_send.at[k, s, pl.ds(0, NY - 1)])
        take(wx_r.at[s], gx_send.at[k, s])

        def residual(slot, _):
            at = pl.ds(pl.multiple_of(slot * tokens, tokens), tokens)
            out = dot(x_all[k, at, :], w_all[k, s])
            res[at, :] = (out - y_all[k, s, slot].astype(F32)).astype(BF16)
            return 0

        lax.fori_loop(0, NY, residual, 0, unroll=True)

        def term(which, b):
            at = pl.multiple_of(which * half + b * rows, rows)
            return dot(x_turn[k, pl.ds(at, rows), :], res[...])

        def theirs(b, _):
            gx_send[k, s, b] = term(other, b).astype(BF16)
            return 0

        def ours(b, _):
            own[s, b] = term(side, b)
            return 0

        lax.fori_loop(0, NY, theirs, 0, unroll=True)
        send(gx_send.at[k, s], gx_recv.at[k, s], gx_s, gx_r.at[s], across)
        lax.fori_loop(0, NY, ours, 0, unroll=True)

    def add(k, s):
        take(gx_r.at[s], gx_recv.at[k, s])
        for b in range(NY):
            gy_send[k, s, b] = (own[s, b] + gx_recv[k, s, b].astype(F32)).astype(BF16)
        for device, place in peers:
            send(gy_send.at[k, s, place], gy_recv.at[k, s, spot], gy_s, gy_r.at[s], device)
        gy_recv[k, s, spot] = gy_send[k, s, spot]

    def expand(c):
        return dot(jnp.concatenate([c, c], axis=1), e[...])

    wide = 256

    def update(k, s):
        take(gy_r.at[s], gy_send.at[k, s, pl.ds(0, NY - 1)])

        @pl.when(jnp.logical_and(k == 0, s == 0))
        def _():
            take(in_sem.at[S], mean)
            take(in_sem.at[S + 1], square)

        for j in range(chunk // wide):
            cols = slice(j * wide, (j + 1) * wide)
            per = wide // part
            grad = jnp.concatenate([gy_recv[k, s, j * per + q] for q in range(per)], axis=1)
            grad = grad.astype(F32) * factor
            mean_next = beta_mean * mean[s, :, cols].astype(F32) + (1.0 - beta_mean) * grad
            square_next = beta_square * square[s, :, cols].astype(F32) + (1.0 - beta_square) * grad * grad
            mean[s, :, cols] = mean_next.astype(BF16)
            square[s, :, cols] = square_next.astype(BF16)
            updated = master[s, :, cols] - step_rate * mean_next / (jnp.sqrt(square_next) + epsilon_add)
            carried = updated + left[s, :, cols]
            high = carried.astype(BF16)
            low = (carried - high.astype(F32)).astype(BF16)
            coeffs = (dot(high, ch[...]) + (dot(low, ch[...]) + dot(high, cl[...]))).astype(BF16)
            c_send[k, s, :, j * (wide // 2) : (j + 1) * (wide // 2)] = coeffs
            back = expand(coeffs)
            left[s, :, cols] = carried - back
            master[s, :, cols] = updated - gossip_rate * back
        partner = (partners[0][0] + k * (partners[1][0] - partners[0][0]), z)
        send(c_send.at[k, s], c_recv.at[k, s], c_s, c_r.at[k, s], partner)

        @pl.when(k + 1 == ITERS)
        def _():
            pltpu.make_async_copy(mean.at[s], moment_out.at[:, columns(s)], out_sem.at[1]).start()
            pltpu.make_async_copy(square.at[s], second_out.at[:, columns(s)], out_sem.at[2]).start()

    def gossip(k, s):
        take(c_r.at[k, s], c_recv.at[k, s])
        remote = c_recv[k, s]
        for j in range(chunk // wide):
            cols = slice(j * wide, (j + 1) * wide)
            piece = remote[:, j * (wide // 2) : (j + 1) * (wide // 2)]
            master[s, :, cols] = master[s, :, cols] + gossip_rate * expand(piece)

        @pl.when(k + 1 == ITERS)
        def _():
            pltpu.make_async_copy(master.at[s], params_out.at[:, columns(s)], out_sem.at[0]).start()

        @pl.when(k + 1 < ITERS)
        def _():
            w_first(k + 1, s)

    take(in_sem.at[S + 2], act)
    pick_x(0)
    take(in_sem.at[0], master.at[0])
    pl.semaphore_wait(barrier, len(friends))
    w_first(0, 0)
    x_first(0)
    take(in_sem.at[S + 3], tgt)
    pick_y(0)
    y_first(0, 0)
    turn(0, 0)
    x_second(0, 0)
    x_second(0, 1)

    def more(s, _):
        take(in_sem.at[s], master.at[s])
        w_first(0, s)
        y_first(0, s)
        return 0

    lax.fori_loop(1, S, more, 0)
    pick_x(1)
    pick_y(1)
    turn(1, 0)

    stages = [w_second, work, add, update, gossip]
    count = len(stages) * ITERS

    def slot(t, _):
        @pl.when(t == 2)
        def _():
            x_first(1)

        @pl.when(t == 4)
        def _():
            x_second(1, 0)
            lax.fori_loop(0, S, lambda s, _: (y_first(1, s), 0)[1], 0)

        @pl.when(t == 5)
        def _():
            x_second(1, 1)

        def visit(r, _):
            s = S - 1 - r
            at = t - s
            for n, stage in enumerate(stages):
                @pl.when(jnp.logical_and(jnp.logical_and(at >= 0, at < count), lax.rem(at, len(stages)) == n))
                def _(stage=stage):
                    stage(lax.div(at, len(stages)), s)

            return 0

        lax.fori_loop(0, S, visit, 0)
        return 0

    lax.fori_loop(0, count + S - 1, slot, 0)

    take(xa_s, x_all.at[:, pl.ds(0, 3 * tokens)])
    take(ya_s, y_send.at[:, :, pl.ds(0, NY - 1)])
    take(wy_s, w_send.at[:, :, pl.ds(0, NY - 1)])
    take(wx_s, gx_send)
    take(gx_s, gx_send)
    take(gy_s, gy_send.at[:, :, pl.ds(0, NY - 1)])
    take(c_s, c_recv)
    take(out_sem.at[0], master)
    take(out_sem.at[1], mean)
    take(out_sem.at[2], square)


def window(bits, cid, params, moment, second, active, target, ids, tables):
    rows, width = params.shape
    depth = active.shape[1]
    tokens = ids.shape[2]
    chunk = width // S
    part = chunk // NY
    group = tokens * NY
    vmem = pl.BlockSpec(memory_space=pltpu.VMEM)
    anywhere = pl.BlockSpec(memory_space=pl.ANY)
    k = ITERS
    dma = pltpu.SemaphoreType.DMA
    scratch = [
        pltpu.VMEM(active.shape, BF16),
        pltpu.VMEM(target.shape, BF16),
        pltpu.VMEM((S, rows, chunk), F32),
        pltpu.VMEM((S, rows, chunk), BF16),
        pltpu.VMEM((S, rows, chunk), BF16),
        pltpu.VMEM((S, rows, chunk), F32),
        pltpu.VMEM((k, group, depth), BF16),
        pltpu.VMEM((k, depth, group), BF16),
        pltpu.VMEM((k, S, NY, tokens, part), BF16),
        pltpu.VMEM((k, S, NY, tokens, part), BF16),
        pltpu.VMEM((k, S, NY, rows, part), BF16),
        pltpu.VMEM((k, S, depth, part), BF16),
        pltpu.VMEM((group, part), BF16),
        pltpu.VMEM((S, NY, rows, part), F32),
        pltpu.VMEM((k, S, NY, rows, part), BF16),
        pltpu.VMEM((k, S, NY, rows, part), BF16),
        pltpu.VMEM((k, S, NY, rows, part), BF16),
        pltpu.VMEM((k, S, NY, rows, part), BF16),
        pltpu.VMEM((k, S, rows, chunk // 2), BF16),
        pltpu.VMEM((k, S, rows, chunk // 2), BF16),
        dma((S + 4,)),
        dma((3,)),
    ]
    for shape in ((k, 4), (k, S), (S,), (S,), (S,), (S,), (k, S)):
        scratch += [dma, dma(shape)]
    return pl.pallas_call(
        functools.partial(kernel, bits),
        out_shape=(
            pltpu.VMEM(params.shape, F32),
            pltpu.VMEM(moment.shape, BF16),
            pltpu.VMEM(second.shape, BF16),
        ),
        in_specs=[anywhere] * 5 + [vmem] * 4,
        out_specs=(vmem,) * 3,
        scratch_shapes=scratch,
        compiler_params=pltpu.CompilerParams(
            collective_id=cid, has_side_effects=True, vmem_limit_bytes=54 * 2**20
        ),
        cost_estimate=pl.CostEstimate(flops=2 * 10**10, bytes_accessed=2 * 10**7, transcendentals=0),
        name=f"window_{cid}",
    )(params, moment, second, active, target, ids, *tables)


def shards(params, moment, second, active, target, row_ids, step_index):
    levels = lax.axis_size("island").bit_length() - 1
    tables = [jnp.asarray(t) for t in cosine_tables()]
    branches = [
        functools.partial(window, tuple((b + k) % levels for k in range(ITERS)), b)
        for b in range(levels)
    ]
    out = lax.switch(
        jnp.remainder(step_index[0], levels),
        branches,
        params[0], moment[0], second[0], active[0], target[0], row_ids, tables,
    )
    return tuple(o[None] for o in out)


def solution(mesh):
    in_specs = (
        P("island", "zero", None),
        P("island", "zero", None),
        P("island", "zero", None),
        P("island", "zero", None),
        P("island", "zero", None),
        P(None, "island", "zero"),
        P(),
    )
    out_specs = (P("island", "zero", None), P("island", "zero", None), P("island", "zero", None))
    return jax.shard_map(shards, mesh=mesh, in_specs=in_specs, out_specs=out_specs, check_vma=False)
```

```python
import functools
import math

import jax
import jax.numpy as jnp
import numpy as np
from jax import lax
from jax.experimental import pallas as pl
from jax.experimental.pallas import tpu as pltpu
from jax.sharding import PartitionSpec as P

MESH = pl.DeviceIdType.MESH
BF16 = jnp.bfloat16
F32 = jnp.float32

ITERS = 2
NY = 4
NX = 2
S = 4

beta_mean = 0.9
beta_square = 0.95
step_rate = 0.02
epsilon_add = 1e-08
gossip_rate = 0.4


def cosine_tables():
    places = np.arange(128)[:, None]
    orders = np.arange(64)[None, :]
    one = np.cos(math.pi * (places + 0.5) * orders / 128.0) * math.sqrt(2.0 / 128.0)
    one = np.where(orders == 0, one * math.sqrt(0.5), one)
    two = np.zeros((256, 128))
    two[:128, :64] = one
    two[128:, 64:] = one
    two = two.astype(np.float32)
    high = two.astype(jnp.bfloat16)
    low = (two - high.astype(np.float32)).astype(jnp.bfloat16)
    return high, low, np.concatenate([high.T, low.T])


def dot(a, b):
    return jnp.dot(a, b, preferred_element_type=F32)


def kernel(
    bits,
    params_in, moment_in, second_in, act_in, tgt_in, ids, ch, cl, e,
    params_out, moment_out, second_out,
    act, tgt, master, mean, square, left, x_all, x_turn, y_send, y_all, w_send, w_all,
    res, own, gx_send, gx_recv, gy_send, gy_recv, c_send, c_recv,
    in_sem, out_sem,
    xa_s, xa_r, ya_s, ya_r, wy_s, wy_r, wx_s, wx_r, gx_s, gx_r, gy_s, gy_r, c_s, c_r,
):
    rows, chunk = master.shape[1:]
    tokens = ids.shape[2]
    stored, depth = act.shape
    part = chunk // NY
    half = depth // NX
    island = lax.axis_index("island")
    z = lax.axis_index("zero")
    factor = 1.0 / math.sqrt(depth * tokens * NX * NY)

    core = lax.rem(island, 2)
    bit_x = lax.rem(z, 2)
    bit_b = lax.div(z, 4)
    bit_a = lax.rem(lax.rem(lax.div(z, 2), 2) + bit_b, 2)
    u = bit_a
    v = bit_b * (1 - core) + bit_x * core
    side = bit_x * (1 - core) + bit_b * core
    spot = 2 * u + v
    other = 1 - side

    def across_edges(a, b, x):
        to_a, to_b, to_x = lax.rem(bit_a + a, 2), lax.rem(bit_b + b, 2), lax.rem(bit_x + x, 2)
        return (island, 4 * to_b + 2 * lax.rem(to_a + to_b, 2) + to_x)

    peers = [
        (across_edges(1, 0, 0), 2 * (1 - u) + v),
        (across_edges(0, 1 - core, core), 2 * u + (1 - v)),
        (across_edges(1, 1 - core, core), 2 * (1 - u) + (1 - v)),
    ]
    across = across_edges(0, core, 1 - core)

    def position(block):
        x = lax.rem(block, 2)
        b = lax.div(block, 4)
        a = lax.rem(lax.rem(lax.div(block, 2), 2) + b, 2)
        return (x * (1 - core) + b * core) * NY + 2 * a + b * (1 - core) + x * core

    partners = []
    for bit in bits:
        apart = 2**bit
        partners.append((island + apart * (1 - 2 * lax.rem(lax.div(island, apart), 2)), z))

    barrier = pltpu.get_barrier_semaphore()
    friends = [device for device, _ in peers] + [across] + partners
    for friend in friends:
        pl.semaphore_signal(barrier, inc=1, device_id=friend, device_id_type=MESH)

    def send(src, dst, s_sem, r_sem, device):
        pltpu.make_async_remote_copy(
            src_ref=src, dst_ref=dst, send_sem=s_sem, recv_sem=r_sem,
            device_id=device, device_id_type=MESH,
        ).start()

    def take(sem, like):
        pltpu.make_async_copy(like, like, sem).wait()

    def columns(s):
        return pl.ds(pl.multiple_of(s * chunk, chunk), chunk)

    pltpu.make_async_copy(act_in, act, in_sem.at[S + 2]).start()
    for s in range(S):
        pltpu.make_async_copy(params_in.at[:, columns(s)], master.at[s], in_sem.at[s]).start()
    for s in range(S):
        pltpu.make_async_copy(moment_in.at[:, columns(s)], mean.at[s], in_sem.at[S]).start()
        pltpu.make_async_copy(second_in.at[:, columns(s)], square.at[s], in_sem.at[S + 1]).start()
    pltpu.make_async_copy(tgt_in, tgt, in_sem.at[S + 3]).start()
    left[...] = jnp.zeros_like(left)

    def selector(k):
        spots = lax.broadcasted_iota(jnp.int32, (stored, tokens), 0)
        return jnp.where(spots == ids[k], 1.0, 0.0).astype(F32).T.astype(BF16)

    def pick_x(k):
        pick = selector(k)

        def step(b, _):
            block = dot(pick, act[:, pl.ds(pl.multiple_of(b * rows, rows), rows)])
            to = position(b) * rows
            x_all[k, 0:tokens, pl.ds(pl.multiple_of(to, rows), rows)] = block.astype(BF16)
            return 0

        lax.fori_loop(0, NX * NY, step, 0, unroll=True)

    def pick_y(k):
        pick = selector(k)

        def step(s, _):
            block = dot(pick, tgt[:, columns(s)]).astype(BF16)
            for q in range(NY):
                y_send[k, s, q] = block[:, q * part : (q + 1) * part]
            return 0

        lax.fori_loop(0, S, step, 0, unroll=True)

    def turn(k, slot):
        def step(b, _):
            at = pl.multiple_of(b * rows, rows)
            block = x_all[k, slot * tokens : (slot + 1) * tokens, pl.ds(at, rows)]
            x_turn[k, pl.ds(at, rows), slot * tokens : (slot + 1) * tokens] = block.T
            return 0

        lax.fori_loop(0, depth // rows, step, 0, unroll=True)

    def x_rows(k, slot, which):
        return x_all.at[k, pl.ds(slot * tokens + which * (tokens // 2), tokens // 2)]

    def x_first(k):
        mine = x_all.at[k, pl.ds(0, tokens)]
        for which in range(2):
            send(x_rows(k, 0, which), x_rows(k, 1, which), xa_s, xa_r.at[k, which], peers[0][0])
        send(mine, x_all.at[k, pl.ds(2 * tokens, tokens)], xa_s, xa_r.at[k, 2], peers[1][0])

    def x_second(k, which):
        take(xa_r.at[k, which], x_rows(k, 1, which))
        send(x_rows(k, 1, which), x_rows(k, 3, which), xa_s, xa_r.at[k, 3], peers[1][0])

    def x_last(k):
        turn(k, 1)
        take(xa_r.at[k, 2], x_all.at[k, pl.ds(0, tokens)])
        turn(k, 2)
        take(xa_r.at[k, 3], x_all.at[k, pl.ds(0, tokens)])
        turn(k, 3)

    def y_first(k, s):
        for n, (device, place) in enumerate(peers):
            send(y_send.at[k, s, place], y_all.at[k, s, n + 1], ya_s, ya_r.at[k, s], device)
        y_all[k, s, 0] = y_send[k, s, spot]

    def w_first(k, s):
        for q in range(NY):
            w_send[k, s, q] = master[s, :, q * part : (q + 1) * part].astype(BF16)
        mine = pl.ds(pl.multiple_of((side * NY + spot) * rows, rows), rows)
        for device, place in peers:
            send(w_send.at[k, s, place], w_all.at[k, s, mine], wy_s, wy_r.at[s], device)
        w_all[k, s, mine] = w_send[k, s, spot]

    def w_second(k, s):
        take(wy_r.at[s], w_send.at[k, s, pl.ds(0, NY - 1)])
        mine = w_all.at[k, s, pl.ds(pl.multiple_of(side * half, half), half)]
        send(mine, mine, wx_s, wx_r.at[s], across)

    def work(k, s):
        @pl.when(s == 0)
        def _():
            x_last(k)

        take(ya_r.at[k, s], y_send.at[k, s, pl.ds(0, NY - 1)])
        take(wx_r.at[s], gx_send.at[k, s])

        def residual(slot, _):
            at = pl.ds(pl.multiple_of(slot * tokens, tokens), tokens)
            out = dot(x_all[k, at, :], w_all[k, s])
            res[at, :] = (out - y_all[k, s, slot].astype(F32)).astype(BF16)
            return 0

        lax.fori_loop(0, NY, residual, 0, unroll=True)

        def term(which, b):
            at = pl.multiple_of(which * half + b * rows, rows)
            return dot(x_turn[k, pl.ds(at, rows), :], res[...])

        def theirs(b, _):
            gx_send[k, s, b] = term(other, b).astype(BF16)
            return 0

        def ours(b, _):
            own[s, b] = term(side, b)
            return 0

        for pair in range(2):
            lax.fori_loop(2 * pair, 2 * pair + 2, theirs, 0, unroll=True)
            two = pl.ds(2 * pair, 2)
            send(gx_send.at[k, s, two], gx_recv.at[k, s, two], gx_s, gx_r.at[s], across)
        lax.fori_loop(0, NY, ours, 0, unroll=True)

    def add(k, s):
        take(gx_r.at[s], gx_recv.at[k, s])
        for b in range(NY):
            gy_send[k, s, b] = (own[s, b] + gx_recv[k, s, b].astype(F32)).astype(BF16)
        for device, place in peers:
            send(gy_send.at[k, s, place], gy_recv.at[k, s, spot], gy_s, gy_r.at[s], device)
        gy_recv[k, s, spot] = gy_send[k, s, spot]

    def expand(c):
        return dot(jnp.concatenate([c, c], axis=1), e[...])

    wide = 256

    def update(k, s):
        take(gy_r.at[s], gy_send.at[k, s, pl.ds(0, NY - 1)])

        @pl.when(jnp.logical_and(k == 0, s == 0))
        def _():
            take(in_sem.at[S], mean)
            take(in_sem.at[S + 1], square)

        partner = (partners[0][0] + k * (partners[1][0] - partners[0][0]), z)
        for j in range(chunk // wide):
            cols = slice(j * wide, (j + 1) * wide)
            per = wide // part
            grad = jnp.concatenate([gy_recv[k, s, j * per + q] for q in range(per)], axis=1)
            grad = grad.astype(F32) * factor
            mean_next = beta_mean * mean[s, :, cols].astype(F32) + (1.0 - beta_mean) * grad
            square_next = beta_square * square[s, :, cols].astype(F32) + (1.0 - beta_square) * grad * grad
            mean[s, :, cols] = mean_next.astype(BF16)
            square[s, :, cols] = square_next.astype(BF16)
            updated = master[s, :, cols] - step_rate * mean_next / (jnp.sqrt(square_next) + epsilon_add)
            carried = updated + left[s, :, cols]
            high = carried.astype(BF16)
            low = (carried - high.astype(F32)).astype(BF16)
            coeffs = (dot(high, ch[...]) + (dot(low, ch[...]) + dot(high, cl[...]))).astype(BF16)
            c_send[k, s, j] = coeffs
            send(c_send.at[k, s, j], c_recv.at[k, s, j], c_s, c_r.at[k, s], partner)
            back = expand(coeffs)
            left[s, :, cols] = carried - back
            master[s, :, cols] = updated - gossip_rate * back

        @pl.when(k + 1 == ITERS)
        def _():
            pltpu.make_async_copy(mean.at[s], moment_out.at[:, columns(s)], out_sem.at[1]).start()
            pltpu.make_async_copy(square.at[s], second_out.at[:, columns(s)], out_sem.at[2]).start()

    def gossip(k, s):
        take(c_r.at[k, s], c_recv.at[k, s])
        for j in range(chunk // wide):
            cols = slice(j * wide, (j + 1) * wide)
            master[s, :, cols] = master[s, :, cols] + gossip_rate * expand(c_recv[k, s, j])

        @pl.when(k + 1 == ITERS)
        def _():
            pltpu.make_async_copy(master.at[s], params_out.at[:, columns(s)], out_sem.at[0]).start()

        @pl.when(k + 1 < ITERS)
        def _():
            w_first(k + 1, s)

    take(in_sem.at[S + 2], act)
    pick_x(0)
    take(in_sem.at[0], master.at[0])
    pl.semaphore_wait(barrier, len(friends))
    w_first(0, 0)
    x_first(0)
    take(in_sem.at[S + 3], tgt)
    pick_y(0)
    y_first(0, 0)
    turn(0, 0)
    x_second(0, 0)
    x_second(0, 1)

    def more(s, _):
        take(in_sem.at[s], master.at[s])
        w_first(0, s)
        y_first(0, s)
        return 0

    lax.fori_loop(1, S, more, 0)
    pick_x(1)
    pick_y(1)
    turn(1, 0)

    stages = [w_second, work, add, update, gossip]
    count = len(stages) * ITERS

    def slot(t, _):
        @pl.when(t == 1)
        def _():
            x_first(1)

        @pl.when(jnp.logical_and(t >= 2, t < S + 2))
        def _():
            y_first(1, t - 2)

        @pl.when(t == 3)
        def _():
            x_second(1, 0)

        @pl.when(t == 4)
        def _():
            x_second(1, 1)

        def visit(r, _):
            s = S - 1 - r
            at = t - s
            for n, stage in enumerate(stages):
                @pl.when(jnp.logical_and(jnp.logical_and(at >= 0, at < count), lax.rem(at, len(stages)) == n))
                def _(stage=stage):
                    stage(lax.div(at, len(stages)), s)

            return 0

        lax.fori_loop(0, S, visit, 0)
        return 0

    lax.fori_loop(0, count + S - 1, slot, 0)

    take(xa_s, x_all.at[:, pl.ds(0, 3 * tokens)])
    take(ya_s, y_send.at[:, :, pl.ds(0, NY - 1)])
    take(wy_s, w_send.at[:, :, pl.ds(0, NY - 1)])
    take(wx_s, gx_send)
    take(gx_s, gx_send)
    take(gy_s, gy_send.at[:, :, pl.ds(0, NY - 1)])
    take(c_s, c_recv)
    take(out_sem.at[0], master)
    take(out_sem.at[1], mean)
    take(out_sem.at[2], square)


def window(bits, cid, params, moment, second, active, target, ids, tables):
    rows, width = params.shape
    depth = active.shape[1]
    tokens = ids.shape[2]
    chunk = width // S
    part = chunk // NY
    group = tokens * NY
    vmem = pl.BlockSpec(memory_space=pltpu.VMEM)
    anywhere = pl.BlockSpec(memory_space=pl.ANY)
    k = ITERS
    dma = pltpu.SemaphoreType.DMA
    scratch = [
        pltpu.VMEM(active.shape, BF16),
        pltpu.VMEM(target.shape, BF16),
        pltpu.VMEM((S, rows, chunk), F32),
        pltpu.VMEM((S, rows, chunk), BF16),
        pltpu.VMEM((S, rows, chunk), BF16),
        pltpu.VMEM((S, rows, chunk), F32),
        pltpu.VMEM((k, group, depth), BF16),
        pltpu.VMEM((k, depth, group), BF16),
        pltpu.VMEM((k, S, NY, tokens, part), BF16),
        pltpu.VMEM((k, S, NY, tokens, part), BF16),
        pltpu.VMEM((k, S, NY, rows, part), BF16),
        pltpu.VMEM((k, S, depth, part), BF16),
        pltpu.VMEM((group, part), BF16),
        pltpu.VMEM((S, NY, rows, part), F32),
        pltpu.VMEM((k, S, NY, rows, part), BF16),
        pltpu.VMEM((k, S, NY, rows, part), BF16),
        pltpu.VMEM((k, S, NY, rows, part), BF16),
        pltpu.VMEM((k, S, NY, rows, part), BF16),
        pltpu.VMEM((k, S, chunk // 256, rows, 128), BF16),
        pltpu.VMEM((k, S, chunk // 256, rows, 128), BF16),
        dma((S + 4,)),
        dma((3,)),
    ]
    for shape in ((k, 4), (k, S), (S,), (S,), (S,), (S,), (k, S)):
        scratch += [dma, dma(shape)]
    return pl.pallas_call(
        functools.partial(kernel, bits),
        out_shape=(
            pltpu.VMEM(params.shape, F32),
            pltpu.VMEM(moment.shape, BF16),
            pltpu.VMEM(second.shape, BF16),
        ),
        in_specs=[anywhere] * 5 + [vmem] * 4,
        out_specs=(vmem,) * 3,
        scratch_shapes=scratch,
        compiler_params=pltpu.CompilerParams(
            collective_id=cid, has_side_effects=True, vmem_limit_bytes=54 * 2**20
        ),
        cost_estimate=pl.CostEstimate(flops=2 * 10**10, bytes_accessed=2 * 10**7, transcendentals=0),
        name=f"window_{cid}",
    )(params, moment, second, active, target, ids, *tables)


def shards(params, moment, second, active, target, row_ids, step_index):
    levels = lax.axis_size("island").bit_length() - 1
    tables = [jnp.asarray(t) for t in cosine_tables()]
    branches = [
        functools.partial(window, tuple((b + k) % levels for k in range(ITERS)), b)
        for b in range(levels)
    ]
    out = lax.switch(
        jnp.remainder(step_index[0], levels),
        branches,
        params[0], moment[0], second[0], active[0], target[0], row_ids, tables,
    )
    return tuple(o[None] for o in out)


def solution(mesh):
    in_specs = (
        P("island", "zero", None),
        P("island", "zero", None),
        P("island", "zero", None),
        P("island", "zero", None),
        P("island", "zero", None),
        P(None, "island", "zero"),
        P(),
    )
    out_specs = (P("island", "zero", None), P("island", "zero", None), P("island", "zero", None))
    return jax.shard_map(shards, mesh=mesh, in_specs=in_specs, out_specs=out_specs, check_vma=False)
```
